32 devices in a mesh: shard: 8 (over y, x, core), rep: 4 (over z).
Axes of the slice: x: 2, y: 2, z: 4, core: 2. Of those that a mesh axis runs over, the one named last changes fastest.
Arguments:
- latents: bfloat16 [384, 256, 384], P(('shard', 'rep')), may hold values from -6 to 6
- labels: int32 [384], P(('shard', 'rep')), may hold values from 0 to 999
- timesteps: int32 [384], P(('shard', 'rep')), may hold values from 0 to 999
- live_counts: int32 [32], P(('shard', 'rep')), may hold values from 1 to 12, as said below
- cotangent: bfloat16 [384, 256, 384], P(('shard', 'rep')), may hold values from -6 to 6
- label_table: bfloat16 [1000, 384], P('shard'), may hold values from -6 to 6
- ada_weight: bfloat16 [384, 2304], P('shard'), may hold values from -0.3125 to 0.3125
- ada_bias: bfloat16 [2304], P('shard'), may hold values from -3 to 3
- qkv_weight: bfloat16 [384, 1152], P('shard'), may hold values from -0.3125 to 0.3125
- qv_bias: bfloat16 [768], P('shard'), may hold values from -3 to 3
- proj_weight: bfloat16 [384, 384], P('shard'), may hold values from -0.875 to 0.875
- proj_bias: bfloat16 [384], P('shard'), may hold values from -3 to 3
- fc1_weight: bfloat16 [384, 1536], P('shard'), may hold values from -0.3125 to 0.3125
- fc1_bias: bfloat16 [1536], P('shard'), may hold values from -3 to 3
- fc2_weight: bfloat16 [1536, 384], P('shard'), may hold values from -0.15625 to 0.15625
- fc2_bias: bfloat16 [384], P('shard'), may hold values from -3 to 3
Outputs:
- block_out: bfloat16 [384, 256, 384], P(('shard', 'rep'))
- latent_grad: float32 [384, 256, 384], P(('shard', 'rep'))
- grad_table: float32 [1000, 384], P('shard')
- grad_ada_weight: float32 [384, 2304], P('shard')
- grad_ada_bias: float32 [2304], P('shard')
- grad_qkv_weight: float32 [384, 1152], P('shard')
- grad_qv_bias: float32 [768], P('shard')
- grad_proj_weight: float32 [384, 384], P('shard')
- grad_proj_bias: float32 [384], P('shard')
- grad_fc1_weight: float32 [384, 1536], P('shard')
- grad_fc1_bias: float32 [1536], P('shard')
- grad_fc2_weight: float32 [1536, 384], P('shard')
- grad_fc2_bias: float32 [384], P('shard')
The draws below stay inside these ranges and needn't reach their ends.
Inputs may be any that keep to these rules, and one draw needn't show every extreme that they name: live_counts[d] latents of device d are live, slots d * 12 to d * 12 + live_counts[d] - 1; some device holds 12.
All inputs are finite; a program needn't handle non-finite values.
Results may differ from the reference program's by a relative error of at most 0.014.
The reference program's roundings to bfloat16 on the way count: a program that leaves them out, or rounds other values in their place, can miss the bound.
Values may be sent and summed in bfloat16 or wider, within the bound.
A program may use at most 128 MiB of HBM per device.

```python
import math
import jax
import jax.numpy as jnp
from jax import lax

D = 384
HEADS = 6
HEAD_DIM = 64
FF = 1536
LABELS = 1000
SEQ = 256
STEPS_T = 1000
SLOTS = 12
LATENTS = 384
N_SHARD = 8
N_REP = 4


def draw_live_counts(key, part):
    first_key, second_key = jax.random.split(key)
    devices_all = N_SHARD * N_REP
    values = jax.random.randint(first_key, (devices_all,), 1, SLOTS + 1)
    fullest = jax.random.randint(second_key, (), 0, devices_all)
    return jnp.where(jnp.arange(devices_all) == fullest, SLOTS, values).astype(jnp.int32)


def touch_ends(drawn, stream_key, low, top_value):
    spot = [jax.random.randint(jax.random.fold_in(stream_key, axis), (), 0, length) for axis, length in enumerate(drawn.shape)]
    widest = drawn.shape.index(max(drawn.shape))
    next_to = spot[:widest] + [(spot[widest] + 1) % drawn.shape[widest]] + spot[widest + 1:]
    return drawn.at[tuple(spot)].set(low).at[tuple(next_to)].set(top_value)


def block_scale(rng, shape, cuts, low, top_value):
    level, own = 1.0, jax.random.fold_in(rng, 6)
    for axis_at, shards_of in cuts:
        steps = jnp.exp(jax.random.uniform(jax.random.fold_in(own, axis_at), (shards_of,), jnp.float32, low / len(cuts), top_value / len(cuts)))
        level = level * jnp.repeat(steps, shape[axis_at] // shards_of).reshape([-1 if axis == axis_at else 1 for axis in range(len(shape))])
    return level


def scatter_about(key, shape, spread, bound, shards=(), kind=jnp.bfloat16):
    array = jax.random.normal(key, shape, jnp.float32) * spread
    if len(shards) > 0:
        array = block_scale(key, shape, shards, -0.22, 0.18) * array
    return jnp.clip(array, min=-bound, max=bound).astype(kind)


def setup_inputs(seed: int = 0) -> dict:
    key_list = jax.random.split(jax.random.key(seed), 17)
    latents = scatter_about(key_list[0], (LATENTS, SEQ, D), 1.0, 6.0, ((0, 32),))
    labels = touch_ends(jax.random.randint(key_list[1], (LATENTS,), 0, LABELS), jax.random.fold_in(key_list[1], 1), 0, LABELS - 1).astype(jnp.int32)
    timesteps = touch_ends(jax.random.randint(key_list[2], (LATENTS,), 0, STEPS_T), jax.random.fold_in(key_list[2], 1), 0, STEPS_T - 1).astype(jnp.int32)
    live_counts = draw_live_counts(jax.random.fold_in(key_list[16], 71), 0)
    cotangent = scatter_about(key_list[4], (LATENTS, SEQ, D), 1.0, 6.0, ((0, 32),))
    label_table = scatter_about(key_list[5], (LABELS, D), 1.0, 6.0, ((0, 8),))
    ada_weight = scatter_about(key_list[6], (D, 6 * D), D ** -0.5, 0.3125, ((0, 8),))
    ada_bias = scatter_about(key_list[7], (6 * D,), 0.5, 3.0, ((0, 8),))
    qkv_weight = scatter_about(key_list[8], (D, 3 * D), D ** -0.5, 0.3125, ((0, 8),))
    qv_bias = scatter_about(key_list[9], (2 * D,), 0.5, 3.0, ((0, 8),))
    proj_weight = scatter_about(key_list[10], (D, D), (D // 8) ** -0.5, 0.875, ((0, 8),))
    proj_bias = scatter_about(key_list[11], (D,), 0.5, 3.0, ((0, 8),))
    fc1_weight = scatter_about(key_list[12], (D, FF), D ** -0.5, 0.3125, ((0, 8),))
    fc1_bias = scatter_about(key_list[13], (FF,), 0.5, 3.0, ((0, 8),))
    fc2_weight = scatter_about(key_list[14], (FF, D), FF ** -0.5, 0.15625, ((0, 8),))
    fc2_bias = scatter_about(key_list[15], (D,), 0.5, 3.0, ((0, 8),))
    return {"latents": latents, "labels": labels, "timesteps": timesteps, "live_counts": live_counts, "cotangent": cotangent, "label_table": label_table, "ada_weight": ada_weight, "ada_bias": ada_bias, "qkv_weight": qkv_weight, "qv_bias": qv_bias, "proj_weight": proj_weight, "proj_bias": proj_bias, "fc1_weight": fc1_weight, "fc1_bias": fc1_bias, "fc2_weight": fc2_weight, "fc2_bias": fc2_bias}


@jax.custom_vjp
def low(v):
    return lax.optimization_barrier(v.astype(jnp.bfloat16)).astype(jnp.float32)

@jax.custom_vjp
def low_back(v):
    return v

def low_keep(v):
    return (low(v), None)

def low_pass(kept, grad):
    return (grad,)

def back_keep(v):
    return (v, None)

def back_low(kept, grad):
    return (low(grad),)
low.defvjp(low_keep, low_pass)
low_back.defvjp(back_keep, back_low)
eps_norm = 1e-06
highest = lax.Precision.HIGHEST

def time_angles(step_ids, model_width):
    half_width = model_width // 2
    frequency = jnp.exp(-math.log(10000.0) * jnp.arange(half_width, dtype=jnp.float32) / half_width)
    angles = step_ids.astype(jnp.float32)[:, None] * frequency[None, :]
    return jnp.concatenate([jnp.cos(angles), jnp.sin(angles)], axis=1)

def normalize_rows(values):
    row_mean = lax.optimization_barrier(jnp.mean(values, axis=-1, keepdims=True))
    centred = values - row_mean
    return centred * lax.rsqrt(lax.optimization_barrier(jnp.mean(centred * centred, axis=-1, keepdims=True)) + eps_norm)

def diffusion_transformer_block(parameter_tree, block_latent_input, block_class_labels, block_timestep_values):
    class_table, ada_mat, ada_vec, qkv_mat, qv_vec, proj_mat, proj_vec, up_mat, up_vec, down_mat, down_vec = parameter_tree
    latent_count, seq_len, model_width = block_latent_input.shape
    head_scale = 1.0 / math.sqrt(HEAD_DIM)
    onehot = (block_class_labels[:, None] == jnp.arange(class_table.shape[0], dtype=jnp.int32)[None, :]).astype(jnp.float32)
    condition = jnp.dot(onehot, class_table, precision=highest) + time_angles(block_timestep_values, model_width)
    cond_act = low(jax.nn.silu(condition))
    modulation = low_back(jnp.dot(cond_act, ada_mat, precision=highest) + ada_vec)
    mod_parts = [modulation[:, piece * model_width:(piece + 1) * model_width][:, None, :] for piece in range(6)]
    shift_a, scale_a, gate_a, shift_b, scale_b, gate_b = mod_parts
    hidden_a = low(normalize_rows(block_latent_input) * (1.0 + scale_a) + shift_a)
    projected = jnp.einsum('bsd,de->bse', hidden_a, qkv_mat, precision=highest)
    query_rows = low(low_back(projected[..., :model_width] + qv_vec[:model_width]))
    key_rows = low(low_back(projected[..., model_width:2 * model_width]))
    value_rows = low(low_back(projected[..., 2 * model_width:] + qv_vec[model_width:]))
    head_shape = (latent_count, seq_len, HEADS, HEAD_DIM)
    scores = low_back(jnp.einsum('bqhd,bkhd->bhqk', query_rows.reshape(head_shape), key_rows.reshape(head_shape), precision=highest) * head_scale)
    expo_scores = jnp.exp(scores - lax.optimization_barrier(jnp.max(scores, axis=-1, keepdims=True)))
    attention = low(expo_scores / lax.optimization_barrier(jnp.sum(expo_scores, axis=-1, keepdims=True)))
    mixed = low(low_back(jnp.einsum('bhqk,bkhd->bqhd', attention, value_rows.reshape(head_shape), precision=highest).reshape(block_latent_input.shape)))
    attn_out = low_back(jnp.einsum('bsd,de->bse', mixed, proj_mat, precision=highest) + proj_vec)
    residual = block_latent_input + gate_a * attn_out
    hidden_b = low(normalize_rows(residual) * (1.0 + scale_b) + shift_b)
    pre_act = low_back(jnp.einsum('bsd,df->bsf', hidden_b, up_mat, precision=highest) + up_vec)
    activated = low(jax.nn.gelu(pre_act, approximate=True))
    mlp_out = low_back(jnp.einsum('bsf,fd->bsd', activated, down_mat, precision=highest) + down_vec)
    return residual + gate_b * mlp_out

def reference(latents, labels, timesteps, live_counts, cotangent, label_table, ada_weight, ada_bias, qkv_weight, qv_bias, proj_weight, proj_bias, fc1_weight, fc1_bias, fc2_weight, fc2_bias):
    parameter_tree = tuple((weight_item.astype(jnp.float32) for weight_item in (label_table, ada_weight, ada_bias, qkv_weight, qv_bias, proj_weight, proj_bias, fc1_weight, fc1_bias, fc2_weight, fc2_bias)))
    groups = LATENTS // SLOTS
    slot_ids = jnp.arange(LATENTS, dtype=jnp.int32)
    live_mask = (slot_ids % SLOTS < live_counts[slot_ids // SLOTS]).astype(jnp.float32)

    def grouped(values):
        return values.reshape((groups, SLOTS) + values.shape[1:])
    inputs = grouped(latents.astype(jnp.float32))
    block_items = (grouped(labels), grouped(timesteps), grouped(live_mask), grouped(cotangent.astype(jnp.float32)))

    def loss_of(weights_float_copy, inputs_f):

        def scan_step(total, block_item):
            block_latent_input, block_class_labels, block_timestep_values, block_mask, block_cot = block_item
            block_latent_output = diffusion_transformer_block(weights_float_copy, block_latent_input, block_class_labels, block_timestep_values)
            masked = block_mask[:, None, None] * block_latent_output
            return (total + jnp.sum(masked * block_cot), masked)
        total, outputs = lax.scan(jax.checkpoint(scan_step), jnp.zeros((), jnp.float32), (inputs_f,) + block_items)
        return (total, outputs)
    total, back_fn, outputs = jax.vjp(loss_of, parameter_tree, inputs, has_aux=True)
    weight_grads, input_grad = back_fn(jnp.ones((), jnp.float32))
    factor = 1.0 / math.sqrt(LATENTS * SEQ)
    block_out = outputs.reshape(latents.shape).astype(jnp.bfloat16)
    latent_grad = input_grad.reshape(latents.shape)
    scaled = [grad_item * factor for grad_item in weight_grads]
    return (block_out, latent_grad, scaled[0], scaled[1], scaled[2], scaled[3], scaled[4], scaled[5], scaled[6], scaled[7], scaled[8], scaled[9], scaled[10])
```

```python
from functools import partial
import math

import jax
import jax.numpy as jnp
from jax import lax
from jax.experimental import pallas as pl
from jax.experimental.pallas import tpu as pltpu
from jax.sharding import PartitionSpec as P

HEAD_DIM = 64
GROUP = 2
EPS = 1e-06
F32 = jnp.float32
BF16 = jnp.bfloat16


def time_angles(step_ids, model_width):
    half_width = model_width // 2
    frequency = jnp.exp(-math.log(10000.0) * jnp.arange(half_width, dtype=F32) / half_width)
    angles = step_ids.astype(F32)[:, None] * frequency[None, :]
    return jnp.concatenate([jnp.cos(angles), jnp.sin(angles)], axis=1)


def normalize(values):
    row_mean = jnp.mean(values, axis=-1, keepdims=True)
    centred = values - row_mean
    inv_std = lax.rsqrt(jnp.mean(centred * centred, axis=-1, keepdims=True) + EPS)
    return centred * inv_std, inv_std


def norm_back(upstream, normed, inv_std):
    return inv_std * (
        upstream
        - jnp.mean(upstream, axis=-1, keepdims=True)
        - normed * jnp.mean(upstream * normed, axis=-1, keepdims=True)
    )


def nn(a, b):
    return lax.dot_general(a, b, (((1,), (0,)), ((), ())), preferred_element_type=F32)


def nt(a, b):
    return lax.dot_general(a, b, (((1,), (1,)), ((), ())), preferred_element_type=F32)


def tn(a, b):
    return lax.dot_general(a, b, (((0,), (0,)), ((), ())), preferred_element_type=F32)


def block_kernel(
    live_ref, x_ref, cot_ref, mods_ref, wqkv, bqv, wproj, bproj, w1, b1, w2, b2,
    out_ref, dx_ref, dmods_ref, gqkv, gproj, g1, g2, gb,
    aqkv, aproj, a1, a2t, ab, probs_s, gelu_s, *, factor,
):
    step = pl.program_id(0)
    group, seq, width = x_ref.shape
    rows = group * seq
    pairs = width // (2 * HEAD_DIM)
    live = live_ref[0]
    base = step * group

    @pl.when(step == 0)
    def _():
        for acc in (aqkv, aproj, a1, a2t, ab):
            acc[...] = jnp.zeros_like(acc)

    @pl.when(base >= live)
    def _():
        out_ref[...] = jnp.zeros_like(out_ref)
        dx_ref[...] = jnp.zeros_like(dx_ref)
        dmods_ref[...] = jnp.zeros_like(dmods_ref)

    @pl.when(base < live)
    def _():
        masks = [jnp.where(base + i < live, 1.0, 0.0).astype(F32) for i in range(group)]

        def mod(piece):
            return jnp.concatenate(
                [
                    jnp.broadcast_to(mods_ref[i, piece : piece + 1, :], (seq, width))
                    for i in range(group)
                ],
                axis=0,
            )

        def by_latent(values, piece):
            for i in range(group):
                dmods_ref[i, piece : piece + 1, :] = jnp.sum(
                    values[i * seq : (i + 1) * seq], axis=0, keepdims=True
                )

        lane = lax.broadcasted_iota(jnp.int32, (1, 2 * HEAD_DIM), 1)
        m0 = jnp.where(lane < HEAD_DIM, 1.0, 0.0).astype(BF16)
        m1 = jnp.where(lane < HEAD_DIM, 0.0, 1.0).astype(BF16)

        def split(pair):
            return jnp.concatenate([pair * m0, pair * m1], axis=0)

        x = x_ref[...].reshape(rows, width).astype(F32)
        normed_a, inv_a = normalize(x)
        hidden_a = (normed_a * (1.0 + mod(1)) + mod(0)).astype(BF16)
        proj = nn(hidden_a, wqkv[...])
        q8 = (proj[:, :width] + bqv[:, :width]).astype(BF16) * jnp.asarray(0.125, BF16)
        k = proj[:, width : 2 * width].astype(BF16)
        v = (proj[:, 2 * width :] + bqv[:, width:]).astype(BF16)

        mixed_rows = []
        for i in range(group):
            r = slice(i * seq, (i + 1) * seq)
            cols = []
            for p in range(pairs):
                c = slice(p * 2 * HEAD_DIM, (p + 1) * 2 * HEAD_DIM)
                s = nt(split(q8[r, c]), k[r, c])
                e = jnp.exp(s - jnp.max(s, axis=-1, keepdims=True))
                pf = e * (1.0 / jnp.sum(e, axis=-1, keepdims=True))
                probs_s[i * pairs + p] = pf
                pb = pf.astype(BF16)
                wide = jnp.concatenate([pb[:seq], pb[seq:]], axis=1)
                cols.append(nn(wide, split(v[r, c])).astype(BF16))
            mixed_rows.append(jnp.concatenate(cols, axis=1))
        mixed = jnp.concatenate(mixed_rows, axis=0)

        attn_out = nn(mixed, wproj[...]) + bproj[...]
        resid = x + mod(2) * attn_out
        normed_b, inv_b = normalize(resid)
        hidden_b = (normed_b * (1.0 + mod(4)) + mod(3)).astype(BF16)
        pre = nn(hidden_b, w1[...]) + b1[...]
        c0 = math.sqrt(2.0 / math.pi)
        sq = pre * pre
        t = jnp.tanh(pre * (c0 + (c0 * 0.044715) * sq))
        half = 0.5 + 0.5 * t
        activ = (pre * half).astype(BF16)
        gelu_s[...] = half + (pre * half) * (1.0 - t) * (c0 + (c0 * 3.0 * 0.044715) * sq)
        mlp_out = nn(activ, w2[...]) + b2[...]

        gate_b = mod(5)
        y = resid + gate_b * mlp_out
        g = []
        for i in range(group):
            r = slice(i * seq, (i + 1) * seq)
            out_ref[i] = (masks[i] * y[r]).astype(BF16)
            g.append(cot_ref[i].astype(F32) * masks[i])
        g = jnp.concatenate(g, axis=0)
        by_latent(g * mlp_out, 5)
        d_mlp = (g * gate_b).astype(BF16)
        ones = jnp.ones((8, rows), BF16)
        a2t[...] += tn(d_mlp, activ)
        d_pre = (nt(d_mlp, w2[...]) * gelu_s[...]).astype(BF16)
        a1[...] += tn(hidden_b, d_pre)
        d_hidden_b = nt(d_pre, w1[...])
        by_latent(d_hidden_b, 3)
        by_latent(d_hidden_b * normed_b, 4)
        d_resid = g + norm_back(d_hidden_b * (1.0 + mod(4)), normed_b, inv_b)
        by_latent(d_resid * attn_out, 2)
        d_attn = (d_resid * mod(2)).astype(BF16)
        aproj[...] += tn(mixed, d_attn)
        d_mixed = nt(d_attn, wproj[...]).astype(BF16)

        dq_rows, dk_rows, dv_rows = [], [], []
        for i in range(group):
            r = slice(i * seq, (i + 1) * seq)
            dq, dk, dv = [], [], []
            for p in range(pairs):
                c = slice(p * 2 * HEAD_DIM, (p + 1) * 2 * HEAD_DIM)
                dm = split(d_mixed[r, c])
                pf = probs_s[i * pairs + p]
                dv.append(tn(pf.astype(BF16), dm).astype(BF16))
                dp = nt(dm, v[r, c])
                ds = (pf * (dp - jnp.sum(dp * pf, axis=-1, keepdims=True))).astype(BF16)
                wide = jnp.concatenate([ds[:seq], ds[seq:]], axis=1)
                dq.append((0.125 * nn(wide, split(k[r, c]))).astype(BF16))
                dk.append(tn(ds, split(q8[r, c])).astype(BF16))
            dq_rows.append(jnp.concatenate(dq, axis=1))
            dk_rows.append(jnp.concatenate(dk, axis=1))
            dv_rows.append(jnp.concatenate(dv, axis=1))
        d_proj = jnp.concatenate(
            [jnp.concatenate(part, axis=0) for part in (dq_rows, dk_rows, dv_rows)], axis=1
        )
        aqkv[...] += tn(hidden_a, d_proj)
        ab[...] += jnp.concatenate(
            [nn(ones, d_proj), nn(ones, d_attn), nn(ones, d_pre), nn(ones, d_mlp)], axis=1
        )
        d_hidden_a = nt(d_proj, wqkv[...])
        by_latent(d_hidden_a, 0)
        by_latent(d_hidden_a * normed_a, 1)
        dx = d_resid + norm_back(d_hidden_a * (1.0 + mod(1)), normed_a, inv_a)
        dx_ref[...] = dx.reshape(group, seq, width)

    @pl.when(step == pl.num_programs(0) - 1)
    def _():
        gqkv[...] = (aqkv[...] * factor).astype(gqkv.dtype)
        gproj[...] = (aproj[...] * factor).astype(gproj.dtype)
        g1[...] = (a1[...] * factor).astype(g1.dtype)
        g2[...] = (a2t[...] * factor).T.astype(g2.dtype)
        gb[...] = ab[...] * factor


def run_block(live, x, cot, mods, wqkv, bqv, wproj, bproj, w1, b1, w2, b2, factor):
    slots, seq, width = x.shape
    ff = w1.shape[1]
    group = GROUP
    pairs = width // (2 * HEAD_DIM)
    nb = 3 * width + width + ff + width
    rows = group * seq
    tokens = lambda: pl.BlockSpec((group, seq, width), lambda i, _: (i, 0, 0))
    six = lambda: pl.BlockSpec((group, 6, width), lambda i, _: (i, 0, 0))
    whole = lambda a: pl.BlockSpec(a.shape, lambda i, _: (0, 0))
    fixed = lambda *s: pl.BlockSpec(s, lambda i, _: (0, 0))
    weights = (wqkv, bqv, wproj, bproj, w1, b1, w2, b2)
    mac = slots * seq * (width * (4 * width + 2 * ff) * 3 + 6 * 4 * seq * width)
    return pl.pallas_call(
        partial(block_kernel, factor=factor),
        grid_spec=pltpu.PrefetchScalarGridSpec(
            num_scalar_prefetch=1,
            grid=(slots // group,),
            in_specs=[tokens(), tokens(), six()] + [whole(w) for w in weights],
            out_specs=[
                tokens(), tokens(), six(),
                fixed(width, 3 * width), fixed(width, width), fixed(width, ff), fixed(ff, width),
                fixed(8, nb),
            ],
            scratch_shapes=[
                pltpu.VMEM((width, 3 * width), F32),
                pltpu.VMEM((width, width), F32),
                pltpu.VMEM((width, ff), F32),
                pltpu.VMEM((width, ff), F32),
                pltpu.VMEM((8, nb), F32),
                pltpu.VMEM((group * pairs, 2 * seq, seq), F32),
                pltpu.VMEM((rows, ff), F32),
            ],
        ),
        out_shape=[
            jax.ShapeDtypeStruct(x.shape, BF16),
            jax.ShapeDtypeStruct(x.shape, F32),
            jax.ShapeDtypeStruct((slots, 6, width), F32),
            jax.ShapeDtypeStruct((width, 3 * width), BF16),
            jax.ShapeDtypeStruct((width, width), BF16),
            jax.ShapeDtypeStruct((width, ff), BF16),
            jax.ShapeDtypeStruct((ff, width), BF16),
            jax.ShapeDtypeStruct((8, nb), F32),
        ],
        compiler_params=pltpu.CompilerParams(
            dimension_semantics=("arbitrary",), vmem_limit_bytes=58 * 1024 * 1024
        ),
        cost_estimate=pl.CostEstimate(
            flops=2 * mac, bytes_accessed=slots * seq * width * 10, transcendentals=0
        ),
        name="block",
    )(live, x, cot, mods, *weights)


def body(
    latents, labels, timesteps, live_counts, cotangent,
    label_table, ada_weight, ada_bias, qkv_weight, qv_bias, proj_weight, proj_bias,
    fc1_weight, fc1_bias, fc2_weight, fc2_bias,
):
    slots, seq, width = latents.shape
    n_shard = lax.axis_size("shard")
    place = lax.axis_index("shard")
    table_rows = label_table.shape[0]
    gather = lambda a: lax.all_gather(a, "shard", axis=0, tiled=True)

    group_labels = gather(labels)
    local = group_labels - place * table_rows
    onehot = local[:, None] == jnp.arange(table_rows, dtype=jnp.int32)[None, :]
    rows = jnp.dot(onehot.astype(BF16), label_table, preferred_element_type=F32).astype(BF16)
    rows = lax.psum_scatter(rows, "shard", scatter_dimension=0, tiled=True)

    ada = gather(ada_weight)
    wqkv, wproj, w1, w2 = (gather(a) for a in (qkv_weight, proj_weight, fc1_weight, fc2_weight))
    sizes = [a.shape[0] for a in (ada_bias, qv_bias, proj_bias, fc1_bias, fc2_bias)]
    packed = lax.all_gather(
        jnp.concatenate([ada_bias, qv_bias, proj_bias, fc1_bias, fc2_bias]), "shard", axis=0
    )
    biases, at = [], 0
    for size in sizes:
        biases.append(packed[:, at : at + size].reshape(1, -1).astype(F32))
        at += size
    ada_b, qv_b, proj_b, fc1_b, fc2_b = biases

    condition = rows.astype(F32) + time_angles(timesteps, width)
    sigmoid_c = jax.nn.sigmoid(condition)
    act = (condition * sigmoid_c).astype(BF16)
    mods = jnp.dot(act, ada, preferred_element_type=F32) + ada_b
    factor = 1.0 / math.sqrt(slots * n_shard * lax.axis_size("rep") * seq)

    block_out, latent_grad, d_mods, gqkv, gproj, g1, g2, gb = run_block(
        live_counts, latents, cotangent, mods.reshape(slots, 6, width),
        wqkv, qv_b, wproj, proj_b, w1, fc1_b, w2, fc2_b, factor,
    )

    d_mods = d_mods.reshape(slots, 6 * width).astype(BF16)
    d_act = lax.dot_general(d_mods, ada, (((1,), (1,)), ((), ())), preferred_element_type=F32)
    d_cond = d_act * sigmoid_c * (1.0 + condition * (1.0 - sigmoid_c))
    group_act = gather(act)
    group_mods = gather(d_mods)
    group_cond = gather(d_cond)
    depth = ada_weight.shape[0]
    my_act = lax.dynamic_slice_in_dim(group_act, place * depth, depth, 1)
    g_ada = lax.dot_general(
        my_act, group_mods, (((0,), (0,)), ((), ())), preferred_element_type=F32
    )
    n_ada = ada_bias.shape[0]
    g_ada_b = jnp.sum(
        lax.dynamic_slice_in_dim(group_mods, place * n_ada, n_ada, 1).astype(F32), axis=0
    )
    g_table = lax.dot_general(
        onehot.astype(F32), group_cond, (((0,), (0,)), ((), ())),
        precision=lax.Precision.HIGHEST, preferred_element_type=F32,
    )
    scatter = lambda a: lax.psum_scatter(a, "shard", scatter_dimension=0, tiled=True)
    gqkv, gproj, g1, g2 = (scatter(a) for a in (gqkv, gproj, g1, g2))
    summed = lax.psum(
        (gqkv, gproj, g1, g2), "rep"
    )
    gqkv, gproj, g1, g2 = (a.astype(F32) for a in summed)
    g_table, g_ada, g_ada_b = lax.psum(
        (g_table * factor, g_ada * factor, g_ada_b * factor), "rep"
    )
    gb = lax.psum(gb[0], ("shard", "rep"))
    ff = fc1_weight.shape[1]
    own = lambda a: lax.dynamic_slice_in_dim(a, place * (a.shape[0] // n_shard), a.shape[0] // n_shard, 0)
    g_qv = own(jnp.concatenate([gb[:width], gb[2 * width : 3 * width]]))
    g_proj_b = own(gb[3 * width : 4 * width])
    g_fc1_b = own(gb[4 * width : 4 * width + ff])
    g_fc2_b = own(gb[4 * width + ff :])
    return (
        block_out, latent_grad, g_table, g_ada, g_ada_b, gqkv, g_qv, gproj, g_proj_b,
        g1, g_fc1_b, g2, g_fc2_b,
    )


def solution(mesh):
    tokens = P(("shard", "rep"), None, None)
    each = P(("shard", "rep"))
    mat, vec = P("shard", None), P("shard")
    return jax.shard_map(
        body,
        mesh=mesh,
        in_specs=(tokens, each, each, each, tokens, mat, mat, vec, mat, vec, mat, vec, mat, vec, mat, vec),
        out_specs=(tokens, tokens, mat, mat, vec, mat, vec, mat, vec, mat, vec, mat, vec),
        check_vma=False,
    )
```

```python
from functools import partial
import math

import jax
import jax.numpy as jnp
from jax import lax
from jax.experimental import pallas as pl
from jax.experimental.pallas import tpu as pltpu
from jax.sharding import PartitionSpec as P

HEAD_DIM = 64
GROUP = 2
EPS = 1e-06
F32 = jnp.float32
BF16 = jnp.bfloat16


def time_angles(step_ids, model_width):
    half_width = model_width // 2
    frequency = jnp.exp(-math.log(10000.0) * jnp.arange(half_width, dtype=F32) / half_width)
    angles = step_ids.astype(F32)[:, None] * frequency[None, :]
    return jnp.concatenate([jnp.cos(angles), jnp.sin(angles)], axis=1)


def normalize(values):
    row_mean = jnp.mean(values, axis=-1, keepdims=True)
    centred = values - row_mean
    inv_std = lax.rsqrt(jnp.mean(centred * centred, axis=-1, keepdims=True) + EPS)
    return centred * inv_std, inv_std


def norm_back(upstream, normed, inv_std):
    return inv_std * (
        upstream
        - jnp.mean(upstream, axis=-1, keepdims=True)
        - normed * jnp.mean(upstream * normed, axis=-1, keepdims=True)
    )


def nn(a, b):
    return lax.dot_general(a, b, (((1,), (0,)), ((), ())), preferred_element_type=F32)


def nt(a, b):
    return lax.dot_general(a, b, (((1,), (1,)), ((), ())), preferred_element_type=F32)


def tn(a, b):
    return lax.dot_general(a, b, (((0,), (0,)), ((), ())), preferred_element_type=F32)


def block_kernel(
    live_ref, x_ref, cot_ref, mods_ref, wqkv, bqv, wproj, bproj, w1, b1, w2, b2,
    out_ref, dx_ref, dmods_ref, pack_ref, gb,
    aqkv, aproj, a1, a2t, ab, probs_s, gelu_s, *, factor,
):
    step = pl.program_id(0)
    group, seq, width = x_ref.shape
    rows = group * seq
    pairs = width // (2 * HEAD_DIM)
    live = live_ref[0]
    base = step * group

    @pl.when(step == 0)
    def _():
        for acc in (aqkv, aproj, a1, a2t, ab):
            acc[...] = jnp.zeros_like(acc)

    @pl.when(base >= live)
    def _():
        out_ref[...] = jnp.zeros_like(out_ref)
        dx_ref[...] = jnp.zeros_like(dx_ref)
        dmods_ref[...] = jnp.zeros_like(dmods_ref)

    @pl.when(base < live)
    def _():
        masks = [jnp.where(base + i < live, 1.0, 0.0).astype(F32) for i in range(group)]

        def mod(piece):
            return jnp.concatenate(
                [
                    jnp.broadcast_to(mods_ref[i, piece : piece + 1, :], (seq, width))
                    for i in range(group)
                ],
                axis=0,
            )

        def by_latent(values, piece):
            for i in range(group):
                dmods_ref[i, piece : piece + 1, :] = jnp.sum(
                    values[i * seq : (i + 1) * seq], axis=0, keepdims=True
                )

        lane = lax.broadcasted_iota(jnp.int32, (1, 2 * HEAD_DIM), 1)
        m0 = jnp.where(lane < HEAD_DIM, 1.0, 0.0).astype(BF16)
        m1 = jnp.where(lane < HEAD_DIM, 0.0, 1.0).astype(BF16)

        def split(pair):
            return jnp.concatenate([pair * m0, pair * m1], axis=0)

        x = x_ref[...].reshape(rows, width).astype(F32)
        normed_a, inv_a = normalize(x)
        hidden_a = (normed_a * (1.0 + mod(1)) + mod(0)).astype(BF16)
        proj = nn(hidden_a, wqkv[...])
        q8 = (proj[:, :width] + bqv[:, :width]).astype(BF16) * jnp.asarray(0.125, BF16)
        k = proj[:, width : 2 * width].astype(BF16)
        v = (proj[:, 2 * width :] + bqv[:, width:]).astype(BF16)

        mixed_rows = []
        for i in range(group):
            r = slice(i * seq, (i + 1) * seq)
            cols = []
            for p in range(pairs):
                c = slice(p * 2 * HEAD_DIM, (p + 1) * 2 * HEAD_DIM)
                s = nt(split(q8[r, c]), k[r, c])
                e = jnp.exp(s - jnp.max(s, axis=-1, keepdims=True))
                pf = e * (1.0 / jnp.sum(e, axis=-1, keepdims=True))
                probs_s[i * pairs + p] = pf
                pb = pf.astype(BF16)
                wide = jnp.concatenate([pb[:seq], pb[seq:]], axis=1)
                cols.append(nn(wide, split(v[r, c])).astype(BF16))
            mixed_rows.append(jnp.concatenate(cols, axis=1))
        mixed = jnp.concatenate(mixed_rows, axis=0)

        attn_out = nn(mixed, wproj[...]) + bproj[...]
        resid = x + mod(2) * attn_out
        normed_b, inv_b = normalize(resid)
        hidden_b = (normed_b * (1.0 + mod(4)) + mod(3)).astype(BF16)
        pre = nn(hidden_b, w1[...]) + b1[...]
        c0 = math.sqrt(2.0 / math.pi)
        sq = pre * pre
        t = jnp.tanh(pre * (c0 + (c0 * 0.044715) * sq))
        half = 0.5 + 0.5 * t
        activ = (pre * half).astype(BF16)
        gelu_s[...] = half + (pre * half) * (1.0 - t) * (c0 + (c0 * 3.0 * 0.044715) * sq)
        mlp_out = nn(activ, w2[...]) + b2[...]

        gate_b = mod(5)
        y = resid + gate_b * mlp_out
        g = []
        for i in range(group):
            r = slice(i * seq, (i + 1) * seq)
            out_ref[i] = (masks[i] * y[r]).astype(BF16)
            g.append(cot_ref[i].astype(F32) * masks[i])
        g = jnp.concatenate(g, axis=0)
        by_latent(g * mlp_out, 5)
        d_mlp = (g * gate_b).astype(BF16)
        ones = jnp.ones((8, rows), BF16)
        a2t[...] += tn(d_mlp, activ)
        d_pre = (nt(d_mlp, w2[...]) * gelu_s[...]).astype(BF16)
        a1[...] += tn(hidden_b, d_pre)
        d_hidden_b = nt(d_pre, w1[...])
        by_latent(d_hidden_b, 3)
        by_latent(d_hidden_b * normed_b, 4)
        d_resid = g + norm_back(d_hidden_b * (1.0 + mod(4)), normed_b, inv_b)
        by_latent(d_resid * attn_out, 2)
        d_attn = (d_resid * mod(2)).astype(BF16)
        aproj[...] += tn(mixed, d_attn)
        d_mixed = nt(d_attn, wproj[...]).astype(BF16)

        dq_rows, dk_rows, dv_rows = [], [], []
        for i in range(group):
            r = slice(i * seq, (i + 1) * seq)
            dq, dk, dv = [], [], []
            for p in range(pairs):
                c = slice(p * 2 * HEAD_DIM, (p + 1) * 2 * HEAD_DIM)
                dm = split(d_mixed[r, c])
                pf = probs_s[i * pairs + p]
                dv.append(tn(pf.astype(BF16), dm).astype(BF16))
                dp = nt(dm, v[r, c])
                ds = (pf * (dp - jnp.sum(dp * pf, axis=-1, keepdims=True))).astype(BF16)
                wide = jnp.concatenate([ds[:seq], ds[seq:]], axis=1)
                dq.append((0.125 * nn(wide, split(k[r, c]))).astype(BF16))
                dk.append(tn(ds, split(q8[r, c])).astype(BF16))
            dq_rows.append(jnp.concatenate(dq, axis=1))
            dk_rows.append(jnp.concatenate(dk, axis=1))
            dv_rows.append(jnp.concatenate(dv, axis=1))
        d_proj = jnp.concatenate(
            [jnp.concatenate(part, axis=0) for part in (dq_rows, dk_rows, dv_rows)], axis=1
        )
        aqkv[...] += tn(hidden_a, d_proj)
        ab[...] += jnp.concatenate(
            [nn(ones, d_proj), nn(ones, d_attn), nn(ones, d_pre), nn(ones, d_mlp)], axis=1
        )
        d_hidden_a = nt(d_proj, wqkv[...])
        by_latent(d_hidden_a, 0)
        by_latent(d_hidden_a * normed_a, 1)
        dx = d_resid + norm_back(d_hidden_a * (1.0 + mod(1)), normed_a, inv_a)
        dx_ref[...] = dx.reshape(group, seq, width)

    @pl.when(step == pl.num_programs(0) - 1)
    def _():
        _, chips, depth, _ = pack_ref.shape
        ff = a1.shape[1]
        parts = ff // width
        down = a2t[...].T
        for s in range(2 * chips):
            r = slice(s * depth, (s + 1) * depth)
            cols = [aqkv[r, :], aproj[r, :], a1[r, :]]
            for b in range(parts):
                top = (s * parts + b) * depth
                cols.append(down[top : top + depth])
            pack_ref[s % 2, s // 2] = (jnp.concatenate(cols, axis=1) * factor).astype(BF16)
        gb[...] = ab[...] * factor


def reduce_kernel(
    pack_ref, small_ref, onehot_ref, out_ref, table_ref,
    recv_a, sum_a, recv_b, small_all, ada_s, stage, full, recv_c, red, gath, tab, recv_t,
    sa, ra, ss, rs, sb, rb, sc, rc, sg, rg, st, rt, *, n_shard, n_rep, factor,
):
    place, rep = lax.axis_index("shard"), lax.axis_index("rep")
    core, chip = lax.rem(place, 2), place // 2
    chips, depth = n_shard // 2, pack_ref.shape[2]
    cols = pack_ref.shape[3]
    width = table_ref.shape[1]
    chunk = stage.shape[2]
    mods = 6 * width

    def peer_shard(o):
        return (lax.rem(place + o, n_shard), rep)

    def peer_chip(o):
        return lax.rem(chip + o, chips)

    def peer_rep(o):
        return lax.rem(rep + o, n_rep)

    def copy(src, dst, send, recv, where):
        c = pltpu.make_async_remote_copy(
            src_ref=src, dst_ref=dst, send_sem=send, recv_sem=recv,
            device_id=where, device_id_type=pl.DeviceIdType.MESH,
        )
        c.start()
        return c

    barrier = pltpu.get_barrier_semaphore()
    for o in range(1, n_shard):
        pl.semaphore_signal(barrier, inc=1, device_id=peer_shard(o), device_id_type=pl.DeviceIdType.MESH)
    for o in range(1, n_rep):
        pl.semaphore_signal(
            barrier, inc=1, device_id=(place, peer_rep(o)), device_id_type=pl.DeviceIdType.MESH
        )
    pl.semaphore_wait(barrier, n_shard + n_rep - 2)

    first = copy(pack_ref.at[1 - core], recv_a, sa.at[0], ra.at[0], (chip * 2 + 1 - core, rep))
    smalls = [
        copy(small_ref, small_all.at[o], ss.at[o], rs.at[o], peer_shard(o)) for o in range(1, n_shard)
    ]
    small_all[0] = small_ref[...]
    first.wait()
    sends = []
    for o in range(1, chips):
        q = peer_chip(o)
        sum_a[q] = (pack_ref[core, q].astype(F32) + recv_a[q].astype(F32)).astype(BF16)
        sends.append(
            copy(sum_a.at[q], recv_b.at[o], sb.at[o], rb.at[o], (q * 2 + core, rep))
        )
    total = pack_ref[core, chip].astype(F32) + recv_a[chip].astype(F32)
    for c in smalls:
        c.wait()
    every = small_all[...].reshape(-1, small_all.shape[2])
    ada_s[...] = tn(every[:, mods : mods + width], every[:, :mods]) * factor
    tab[...] = (nn(onehot_ref[...], every[:, mods + width :]) * factor).astype(BF16)
    tabs = [
        copy(tab, recv_t.at[o], st.at[o], rt.at[o], (place, peer_rep(o))) for o in range(1, n_rep)
    ]
    full[...] = jnp.zeros_like(full)
    full[:, cols : cols + mods] = ada_s[pl.ds(pl.multiple_of(place * depth, 16), depth), :]
    for c, o in zip(sends, range(1, chips)):
        c.wait()
        total = total + recv_b[o].astype(F32)
    full[:, :cols] = total
    for j in range(n_rep):
        stage[j] = full[:, j * chunk : (j + 1) * chunk].astype(BF16)
    sends = [
        copy(stage.at[peer_rep(o)], recv_c.at[o], sc.at[o], rc.at[o], (place, peer_rep(o)))
        for o in range(1, n_rep)
    ]
    part = stage[rep].astype(F32)
    for c, o in zip(sends, range(1, n_rep)):
        c.wait()
        part = part + recv_c[o].astype(F32)
    red[...] = part.astype(BF16)
    sends = [
        copy(red, gath.at[o], sg.at[o], rg.at[o], (place, peer_rep(o)))
        for o in range(1, n_rep)
    ]
    out_ref[rep] = red[...]
    table = tab[...].astype(F32)
    for c, o in zip(tabs, range(1, n_rep)):
        c.wait()
        table = table + recv_t[o].astype(F32)
    table_ref[...] = table
    for c, o in zip(sends, range(1, n_rep)):
        c.wait()
        out_ref[lax.rem(rep + n_rep - o, n_rep)] = gath[o]


def reduce_all(pack, small, onehot, n_shard, n_rep, factor):
    _, chips, depth, cols = pack.shape
    width = depth * n_shard
    tiles = (cols + 6 * width) // 128
    chunk = -(-tiles // n_rep) * 128
    sem = lambda n: pltpu.SemaphoreType.DMA((n,))
    vmem = lambda: pl.BlockSpec(memory_space=pltpu.VMEM)
    return pl.pallas_call(
        partial(reduce_kernel, n_shard=n_shard, n_rep=n_rep, factor=factor),
        in_specs=[vmem()] * 3,
        out_specs=[vmem()] * 2,
        out_shape=[
            jax.ShapeDtypeStruct((n_rep, depth, chunk), BF16),
            jax.ShapeDtypeStruct((onehot.shape[0], width), F32),
        ],
        scratch_shapes=[
            pltpu.VMEM((chips, depth, cols), BF16),
            pltpu.VMEM((chips, depth, cols), BF16),
            pltpu.VMEM((chips, depth, cols), BF16),
            pltpu.VMEM((n_shard,) + small.shape, BF16),
            pltpu.VMEM((width, 6 * width), F32),
            pltpu.VMEM((n_rep, depth, chunk), BF16),
            pltpu.VMEM((depth, n_rep * chunk), F32),
            pltpu.VMEM((n_rep, depth, chunk), BF16),
            pltpu.VMEM((depth, chunk), BF16),
            pltpu.VMEM((n_rep, depth, chunk), BF16),
            pltpu.VMEM((onehot.shape[0], width), BF16),
            pltpu.VMEM((n_rep, onehot.shape[0], width), BF16),
            sem(1), sem(1), sem(n_shard), sem(n_shard), sem(chips), sem(chips),
            sem(n_rep), sem(n_rep), sem(n_rep), sem(n_rep), sem(n_rep), sem(n_rep),
        ],
        compiler_params=pltpu.CompilerParams(
            collective_id=1, has_side_effects=True, vmem_limit_bytes=56 * 1024 * 1024
        ),
        cost_estimate=pl.CostEstimate(flops=10**9, bytes_accessed=10**8, transcendentals=0),
        name="reduce",
    )(pack, small, onehot)


def run_block(live, x, cot, mods, wqkv, bqv, wproj, bproj, w1, b1, w2, b2, factor, n_shard):
    slots, seq, width = x.shape
    ff = w1.shape[1]
    group = GROUP
    pairs = width // (2 * HEAD_DIM)
    nb = 3 * width + width + ff + width
    rows = group * seq
    depth = width // n_shard
    packed = (2, n_shard // 2, depth, 4 * width + 2 * ff)
    tokens = lambda: pl.BlockSpec((group, seq, width), lambda i, _: (i, 0, 0))
    six = lambda: pl.BlockSpec((group, 6, width), lambda i, _: (i, 0, 0))
    whole = lambda a: pl.BlockSpec(a.shape, lambda i, _: (0, 0))
    fixed = lambda *s: pl.BlockSpec(s, lambda i, _: (0, 0))
    weights = (wqkv, bqv, wproj, bproj, w1, b1, w2, b2)
    mac = slots * seq * (width * (4 * width + 2 * ff) * 3 + 6 * 4 * seq * width)
    return pl.pallas_call(
        partial(block_kernel, factor=factor),
        grid_spec=pltpu.PrefetchScalarGridSpec(
            num_scalar_prefetch=1,
            grid=(slots // group,),
            in_specs=[tokens(), tokens(), six()] + [whole(w) for w in weights],
            out_specs=[
                tokens(), tokens(), six(),
                pl.BlockSpec(packed, lambda i, _: (0, 0, 0, 0)),
                fixed(8, nb),
            ],
            scratch_shapes=[
                pltpu.VMEM((width, 3 * width), F32),
                pltpu.VMEM((width, width), F32),
                pltpu.VMEM((width, ff), F32),
                pltpu.VMEM((width, ff), F32),
                pltpu.VMEM((8, nb), F32),
                pltpu.VMEM((group * pairs, 2 * seq, seq), F32),
                pltpu.VMEM((rows, ff), F32),
            ],
        ),
        out_shape=[
            jax.ShapeDtypeStruct(x.shape, BF16),
            jax.ShapeDtypeStruct(x.shape, F32),
            jax.ShapeDtypeStruct((slots, 6, width), F32),
            jax.ShapeDtypeStruct(packed, BF16),
            jax.ShapeDtypeStruct((8, nb), F32),
        ],
        compiler_params=pltpu.CompilerParams(
            dimension_semantics=("arbitrary",), vmem_limit_bytes=58 * 1024 * 1024
        ),
        cost_estimate=pl.CostEstimate(
            flops=2 * mac, bytes_accessed=slots * seq * width * 10, transcendentals=0
        ),
        name="block",
    )(live, x, cot, mods, *weights)


def body(
    latents, labels, timesteps, live_counts, cotangent,
    label_table, ada_weight, ada_bias, qkv_weight, qv_bias, proj_weight, proj_bias,
    fc1_weight, fc1_bias, fc2_weight, fc2_bias,
):
    slots, seq, width = latents.shape
    n_shard = lax.axis_size("shard")
    place = lax.axis_index("shard")
    table_rows = label_table.shape[0]
    gather = lambda a: lax.all_gather(a, "shard", axis=0, tiled=True)

    group_labels = gather(labels)
    local = group_labels - place * table_rows
    onehot = local[:, None] == jnp.arange(table_rows, dtype=jnp.int32)[None, :]
    rows = jnp.dot(onehot.astype(BF16), label_table, preferred_element_type=F32).astype(BF16)
    rows = lax.psum_scatter(rows, "shard", scatter_dimension=0, tiled=True)

    ada = gather(ada_weight)
    wqkv, wproj, w1, w2 = (gather(a) for a in (qkv_weight, proj_weight, fc1_weight, fc2_weight))
    sizes = [a.shape[0] for a in (ada_bias, qv_bias, proj_bias, fc1_bias, fc2_bias)]
    packed = lax.all_gather(
        jnp.concatenate([ada_bias, qv_bias, proj_bias, fc1_bias, fc2_bias]), "shard", axis=0
    )
    biases, at = [], 0
    for size in sizes:
        biases.append(packed[:, at : at + size].reshape(1, -1).astype(F32))
        at += size
    ada_b, qv_b, proj_b, fc1_b, fc2_b = biases

    condition = rows.astype(F32) + time_angles(timesteps, width)
    sigmoid_c = jax.nn.sigmoid(condition)
    act = (condition * sigmoid_c).astype(BF16)
    mods = jnp.dot(act, ada, preferred_element_type=F32) + ada_b
    factor = 1.0 / math.sqrt(slots * n_shard * lax.axis_size("rep") * seq)

    block_out, latent_grad, d_mods, pack, gb = run_block(
        live_counts, latents, cotangent, mods.reshape(slots, 6, width),
        wqkv, qv_b, wproj, proj_b, w1, fc1_b, w2, fc2_b, factor, n_shard,
    )

    d_mods = d_mods.reshape(slots, 6 * width).astype(BF16)
    d_act = lax.dot_general(d_mods, ada, (((1,), (1,)), ((), ())), preferred_element_type=F32)
    d_cond = d_act * sigmoid_c * (1.0 + condition * (1.0 - sigmoid_c))
    pad = -slots % 16
    small = jnp.pad(
        jnp.concatenate([d_mods, act, d_cond.astype(BF16)], axis=1), ((0, pad), (0, 0))
    )
    order = (place - jnp.arange(n_shard, dtype=jnp.int32)) % n_shard
    slot_local = jnp.pad(
        jnp.take(local.reshape(n_shard, slots), order, axis=0),
        ((0, 0), (0, pad)), constant_values=-1,
    ).reshape(-1)
    table_pad = table_rows + (-table_rows % 16)
    slot_hot = (
        jnp.arange(table_pad, dtype=jnp.int32)[:, None]
        == jnp.where(slot_local < table_rows, slot_local, -1)[None, :]
    ).astype(BF16)
    vec = jnp.concatenate([gb[0], jnp.sum(d_mods.astype(F32), axis=0) * factor])
    vec = lax.psum(vec, ("shard", "rep"))
    n_rep = lax.axis_size("rep")
    red, g_table = reduce_all(pack, small, slot_hot, n_shard, n_rep, factor)
    g_table = g_table[:table_rows]
    depth = ada_weight.shape[0]
    ff = fc1_weight.shape[1]
    flat = jnp.concatenate([red[j] for j in range(n_rep)], axis=1).astype(F32)
    gqkv = flat[:, : 3 * width]
    gproj = flat[:, 3 * width : 4 * width]
    g1 = flat[:, 4 * width : 4 * width + ff]
    top = 4 * width + ff
    g2 = jnp.concatenate(
        [flat[:, top + b * width : top + (b + 1) * width] for b in range(ff // width)], axis=0
    )
    g_ada = flat[:, top + ff : top + ff + 6 * width]
    own = lambda a: lax.dynamic_slice_in_dim(a, place * (a.shape[0] // n_shard), a.shape[0] // n_shard, 0)
    g_qv = own(jnp.concatenate([vec[:width], vec[2 * width : 3 * width]]))
    g_proj_b = own(vec[3 * width : 4 * width])
    g_fc1_b = own(vec[4 * width : 4 * width + ff])
    g_fc2_b = own(vec[4 * width + ff : 5 * width + ff])
    g_ada_b = own(vec[5 * width + ff :])
    return (
        block_out, latent_grad, g_table, g_ada, g_ada_b, gqkv, g_qv, gproj, g_proj_b,
        g1, g_fc1_b, g2, g_fc2_b,
    )


def solution(mesh):
    tokens = P(("shard", "rep"), None, None)
    each = P(("shard", "rep"))
    mat, vec = P("shard", None), P("shard")
    return jax.shard_map(
        body,
        mesh=mesh,
        in_specs=(tokens, each, each, each, tokens, mat, mat, vec, mat, vec, mat, vec, mat, vec, mat, vec),
        out_specs=(tokens, tokens, mat, mat, vec, mat, vec, mat, vec, mat, vec, mat, vec),
        check_vma=False,
    )
```
